32 devices in a mesh: depth: 8 (over z, y), filt: 4 (over x, core).
Axes of the slice: x: 2, y: 2, z: 4, core: 2. Of those that a mesh axis runs over, the one named last changes fastest.
Arguments:
- features: bfloat16 [16, 128, 4096], P('depth', 'filt'), may hold values from -6 to 6
- first_kernel: bfloat16 [3, 3, 3, 256, 128], P(None, None, None, 'filt'), may hold values from -0.109375 to 0.109375
- first_bias: float32 [256], P('filt'), may hold values from -1.5 to 1.5
- second_kernel: bfloat16 [3, 3, 3, 256, 256], P(None, None, None, 'filt'), may hold values from -0.078125 to 0.078125
- second_bias: float32 [256], P('filt'), may hold values from -1.5 to 1.5
Outputs:
- activated: bfloat16 [16, 256, 4096], P('depth', 'filt')
The draws below stay inside these ranges and needn't reach their ends.
All inputs are finite; a program needn't handle non-finite values.
Results may differ from the reference program's by a relative error of at most 0.0047.
Values may be sent and summed in bfloat16 or wider, within the bound.
A program may use at most 64 MiB of HBM per device.

```python
import jax
import jax.numpy as jnp
from jax import lax

CIN = 128
CMID = 256
COUT = 256
SIDE = 64
DEPTH_CELLS = 16
PLANE_CELLS = 4096


def levels(rng, dims, split, smallest, largest):
    factor_of, own = 1.0, jax.random.fold_in(rng, 6)
    for dim, parts in split:
        steps = jnp.exp(jax.random.uniform(jax.random.fold_in(own, dim), (parts,), jnp.float32, smallest / len(split), largest / len(split)))
        factor_of = factor_of * jnp.repeat(steps, dims[dim] // parts).reshape([-1 if axis == dim else 1 for axis in range(len(dims))])
    return factor_of


def normal_values(own_key, extent, spread, bound, pieces=(), held_as=jnp.bfloat16):
    level = levels(own_key, extent, pieces, -0.22, 0.18) if pieces else 1.0
    values = jax.random.normal(own_key, extent, jnp.float32) * spread * level
    return jnp.minimum(jnp.maximum(values, -bound), bound).astype(held_as)


def setup_inputs(seed: int = 0) -> dict:
    keys = jax.random.split(jax.random.key(seed), 6)
    return {
        "features": normal_values(keys[0], (DEPTH_CELLS, CIN, PLANE_CELLS), 1.0, 6.0, ((0, 8), (1, 4))),
        "first_kernel": normal_values(keys[1], (3, 3, 3, CMID, CIN), (27 * CIN) ** -0.5, 0.109375, ((3, 4),)),
        "first_bias": normal_values(keys[2], (CMID,), 0.3, 1.5, ((0, 4),), jnp.float32),
        "second_kernel": normal_values(keys[3], (3, 3, 3, COUT, CMID), (27 * CMID) ** -0.5, 0.078125, ((3, 4),)),
        "second_bias": normal_values(keys[4], (COUT,), 0.3, 1.5, ((0, 4),), jnp.float32),
    }


leak_slope = 0.3


def convolve(volume_in, kernel):
    planes = volume_in.shape[0]
    channels = volume_in.shape[1]
    cube = volume_in.astype(jnp.float32).reshape(planes, channels, SIDE, SIDE)
    left_side = jnp.transpose(cube, (0, 2, 3, 1))[None]
    right_side = jnp.transpose(kernel.astype(jnp.float32), (0, 1, 2, 4, 3))
    result = lax.conv_general_dilated(left_side, right_side, (1, 1, 1), ((1, 1), (1, 1), (1, 1)), dimension_numbers=("NDHWC", "DHWIO", "NDHWC"), precision=lax.Precision.HIGHEST)
    result = jnp.transpose(result[0], (0, 3, 1, 2))
    return result.reshape(planes, kernel.shape[3], SIDE * SIDE)


def activate(summed, bias):
    shifted = summed + bias.astype(jnp.float32)[None, :, None]
    return jnp.where(shifted > 0, shifted, leak_slope * shifted).astype(jnp.bfloat16)


def reference(features, first_kernel, first_bias, second_kernel, second_bias):
    hidden = activate(convolve(features, first_kernel), first_bias)
    return activate(convolve(hidden, second_kernel), second_bias)
```

```python
import jax
import jax.numpy as jnp
from jax import lax
from jax.sharding import PartitionSpec as P

SIDE = 64
REACH = 2


leak_slope = 0.3


def depth_padded(block, width):
    count = lax.axis_size("depth")
    forward = [(i, i + 1) for i in range(count - 1)]
    backward = [(target, source) for source, target in forward]
    low = lax.ppermute(block[block.shape[0] - width :], "depth", forward)
    high = lax.ppermute(block[:width], "depth", backward)
    return jnp.concatenate([low, block, high], axis=0)


def row_blocks(features, parts, rows):
    framed = jnp.pad(features, ((0, 0), (0, 0), (REACH * SIDE, REACH * SIDE)))
    span = (rows + 2 * REACH) * SIDE
    return jnp.stack(
        [framed[:, :, part * rows * SIDE : part * rows * SIDE + span] for part in range(parts)]
    )


def convolve(volume, kernel):
    return lax.conv_general_dilated(
        volume[None],
        kernel,
        (1, 1, 1),
        ((0, 0), (0, 0), (1, 1)),
        dimension_numbers=("NDHWC", "DHWOI", "NDHWC"),
        preferred_element_type=jnp.float32,
    )[0]


def activate(summed, bias):
    shifted = summed + bias
    return jnp.where(shifted > 0, shifted, leak_slope * shifted)


def inside(count, offset, limit):
    place = jnp.arange(count, dtype=jnp.int32) + offset
    return (place >= 0) & (place < limit)


def local(features, first_kernel, first_bias, second_kernel, second_bias):
    parts = lax.axis_size("filt")
    rows = SIDE // parts
    planes, share = features.shape[0], features.shape[1]
    channels = share * parts
    depth_limit = planes * lax.axis_size("depth")
    first_whole = lax.all_gather(first_kernel, "filt", axis=3, tiled=True)
    second_whole = lax.all_gather(second_kernel, "filt", axis=3, tiled=True)
    first_shift = lax.all_gather(first_bias, "filt", axis=0, tiled=True)
    second_shift = lax.all_gather(second_bias, "filt", axis=0, tiled=True)
    blocks = lax.all_to_all(row_blocks(features, parts, rows), "filt", 0, 0)
    mine = jnp.transpose(blocks, (1, 3, 0, 2)).reshape(planes, -1, channels)
    volume = depth_padded(mine, REACH).reshape(planes + 2 * REACH, rows + 2 * REACH, SIDE, channels)
    first_sum = convolve(volume, first_whole)
    hidden = activate(first_sum, first_shift)
    deep = inside(planes + 2, lax.axis_index("depth") * planes - 1, depth_limit)
    high = inside(rows + 2, lax.axis_index("filt") * rows - 1, SIDE)
    usable = deep[:, None] & high[None, :]
    hidden = jnp.where(usable[:, :, None, None], hidden, 0.0).astype(jnp.bfloat16)
    activated = activate(convolve(hidden, second_whole), second_shift).astype(jnp.bfloat16)
    flat = jnp.transpose(activated.reshape(planes, rows * SIDE, -1), (0, 2, 1))
    return lax.all_to_all(flat, "filt", 1, 2, tiled=True)


def solution(mesh):
    in_specs = (
        P("depth", "filt", None),
        P(None, None, None, "filt", None),
        P("filt"),
        P(None, None, None, "filt", None),
        P("filt"),
    )
    out_specs = P("depth", "filt", None)
    return jax.shard_map(local, mesh=mesh, in_specs=in_specs, out_specs=out_specs, check_vma=False)
```

```python
import jax
import jax.numpy as jnp
from jax import lax
from jax.sharding import PartitionSpec as P

SIDE = 64
REACH = 2
PAIR = 2


leak_slope = 0.3


def depth_padded(block, width):
    count = lax.axis_size("depth")
    forward = [(i, i + PAIR) for i in range(count - PAIR)]
    backward = [(target, source) for source, target in forward]
    low = lax.ppermute(block[block.shape[0] - width :], "depth", forward)
    high = lax.ppermute(block[:width], "depth", backward)
    return jnp.concatenate([low, block, high], axis=0)


def gathered(block):
    count = lax.axis_size("filt")
    place = lax.axis_index("filt")
    stride = count // 2
    block = block[None]
    while stride:
        other = lax.ppermute(block, "filt", [(i, i ^ stride) for i in range(count)])
        upper = (place // stride) % 2 == 1
        block = jnp.where(upper, jnp.stack([other, block], 1), jnp.stack([block, other], 1))
        block = block.reshape((-1,) + block.shape[2:])
        stride //= 2
    return block


def whole_kernel(kernel):
    blocks = gathered(kernel.reshape(27, kernel.shape[3], kernel.shape[4]))
    return jnp.transpose(blocks, (1, 0, 2, 3)).reshape(3, 3, 3, -1, kernel.shape[4])


def row_blocks(features, parts, rows):
    framed = jnp.pad(features, ((0, 0), (0, 0), (REACH * SIDE, REACH * SIDE)))
    span = (rows + 2 * REACH) * SIDE
    return jnp.stack(
        [framed[:, :, part * rows * SIDE : part * rows * SIDE + span] for part in range(parts)]
    )


def convolve(volume, kernel):
    return lax.conv_general_dilated(
        volume[None],
        kernel,
        (1, 1, 1),
        ((0, 0), (0, 0), (1, 1)),
        dimension_numbers=("NDHWC", "DHWOI", "NDHWC"),
        preferred_element_type=jnp.float32,
    )[0]


def activate(summed, bias):
    shifted = summed + bias
    return jnp.where(shifted > 0, shifted, leak_slope * shifted)


def inside(count, offset, limit):
    place = jnp.arange(count, dtype=jnp.int32) + offset
    return (place >= 0) & (place < limit)


def local(features, first_kernel, first_bias, second_kernel, second_bias):
    shares = lax.axis_size("filt")
    parts = PAIR * shares
    rows = SIDE // parts
    share = features.shape[1]
    planes = features.shape[0] * PAIR
    channels = share * shares
    count = lax.axis_size("depth")
    depth_limit = features.shape[0] * count
    groups = [list(range(i * parts, (i + 1) * parts)) for i in range(count // PAIR)]
    where = lax.axis_index("depth")
    part = (where % PAIR) * shares + lax.axis_index("filt")
    first_whole = whole_kernel(first_kernel)
    second_whole = whole_kernel(second_kernel)
    shifts = gathered(jnp.stack([first_bias, second_bias]))
    first_shift, second_shift = shifts[:, 0].reshape(-1), shifts[:, 1].reshape(-1)
    blocks = lax.all_to_all(
        row_blocks(features, parts, rows), ("depth", "filt"), 0, 0, axis_index_groups=groups
    )
    blocks = blocks.reshape(PAIR, shares, features.shape[0], share, -1)
    mine = jnp.transpose(blocks, (0, 2, 4, 1, 3)).reshape(planes, -1, channels)
    volume = depth_padded(mine, REACH).reshape(planes + 2 * REACH, rows + 2 * REACH, SIDE, channels)
    first_sum = convolve(volume, first_whole)
    hidden = activate(first_sum, first_shift)
    deep = inside(planes + 2, (where // PAIR) * planes - 1, depth_limit)
    high = inside(rows + 2, part * rows - 1, SIDE)
    usable = deep[:, None] & high[None, :]
    hidden = jnp.where(usable[:, :, None, None], hidden, 0.0).astype(jnp.bfloat16)
    activated = activate(convolve(hidden, second_whole), second_shift).astype(jnp.bfloat16)
    flat = activated.reshape(PAIR, features.shape[0], rows * SIDE, shares, -1)
    flat = jnp.transpose(flat, (0, 3, 1, 4, 2)).reshape(parts, features.shape[0], -1, rows * SIDE)
    flat = lax.all_to_all(flat, ("depth", "filt"), 0, 0, axis_index_groups=groups)
    return jnp.transpose(flat, (1, 2, 0, 3)).reshape(features.shape[0], -1, SIDE * SIDE)


def solution(mesh):
    in_specs = (
        P("depth", "filt", None),
        P(None, None, None, "filt", None),
        P("filt"),
        P(None, None, None, "filt", None),
        P("filt"),
    )
    out_specs = P("depth", "filt", None)
    return jax.shard_map(local, mesh=mesh, in_specs=in_specs, out_specs=out_specs, check_vma=False)
```

```python
import functools

import jax
import jax.numpy as jnp
from jax import lax
from jax.experimental import pallas as pl
from jax.experimental.pallas import tpu as pltpu
from jax.sharding import PartitionSpec as P

SIDE = 64
REACH = 2
PAIR = 2
MESH = pl.DeviceIdType.MESH


leak_slope = 0.3


def activate(summed, bias):
    shifted = summed + bias
    return jnp.where(shifted > 0, shifted, leak_slope * shifted)


def spread(values, buffer, plane):
    cells, channels = values.shape
    column = lax.broadcasted_iota(jnp.int32, (cells, 1), 0) % SIDE
    before = jnp.where(column > 0, pltpu.roll(values, 1, 0), 0.0)
    after = jnp.where(column < SIDE - 1, pltpu.roll(values, cells - 1, 0), 0.0)
    buffer[plane, :, 0:channels] = before.astype(jnp.bfloat16)
    buffer[plane, :, channels : 2 * channels] = values.astype(jnp.bfloat16)
    buffer[plane, :, 2 * channels : 3 * channels] = after.astype(jnp.bfloat16)


def tap_sum(buffer, kernels, shares, plane, cells):
    total = None
    for tap_d in range(3):
        for tap_h in range(3):
            window = buffer[plane + tap_d, tap_h * SIDE : tap_h * SIDE + cells, :]
            weights = jnp.concatenate(
                [kernels[i, 3 * tap_d + tap_h] for i in range(shares)], axis=0
            )
            term = lax.dot_general(
                window, weights, (((1,), (1,)), ((), ())), preferred_element_type=jnp.float32
            )
            total = term if total is None else total + term
    return total


def kernel(
    shares, count, depth_planes,
    x_ref, k1_ref, k2_ref, b_ref, out_ref,
    held, taps1, taps2, k1_all, k2_all, b_all, results,
    x_send, x_recv, z_send, z_recv, w_send, w_recv, b_send, b_recv, o_send, o_recv, own_sem,
):
    parts = PAIR * shares
    rows = SIDE // parts
    span = (rows + 2 * REACH) * SIDE
    planes = PAIR * depth_planes
    where = lax.axis_index("depth")
    f = lax.axis_index("filt")
    base = (where // PAIR) * PAIR
    side = where % PAIR
    part = side * shares + f
    mate = f + 1 - 2 * (f % 2)
    below = where >= PAIR
    above = where < count - PAIR

    def home(other):
        return (base + other // shares, other % shares)

    barrier = pltpu.get_barrier_semaphore()
    for k in range(1, parts):
        pl.semaphore_signal(barrier, inc=1, device_id=home((part + k) % parts), device_id_type=MESH)

    @pl.when(below)
    def _():
        pl.semaphore_signal(barrier, inc=1, device_id=(where - PAIR, f), device_id_type=MESH)

    @pl.when(above)
    def _():
        pl.semaphore_signal(barrier, inc=1, device_id=(where + PAIR, f), device_id_type=MESH)

    pl.semaphore_wait(barrier, parts - 1 + below.astype(jnp.int32) + above.astype(jnp.int32))

    def x_copy(k):
        to = (part + k) % parts
        return pltpu.make_async_remote_copy(
            src_ref=x_ref.at[:, :, pl.ds(pl.multiple_of(to * rows * SIDE, 128), span)],
            dst_ref=held.at[1 + side, f],
            send_sem=x_send.at[k], recv_sem=x_recv.at[k],
            device_id=home(to), device_id_type=MESH,
        )

    def w_first(layer, ref, dest, m):
        to = mate if m == 0 else (f + 2 * m) % shares
        return pltpu.make_async_remote_copy(
            src_ref=ref, dst_ref=dest.at[f],
            send_sem=w_send.at[layer, 0, m], recv_sem=w_recv.at[layer, 0, m],
            device_id=(where, to), device_id_type=MESH,
        )

    def w_second(layer, dest, m):
        source = (f - 2 * m + shares) % shares
        return pltpu.make_async_remote_copy(
            src_ref=dest.at[source], dst_ref=dest.at[source],
            send_sem=w_send.at[layer, 1, m], recv_sem=w_recv.at[layer, 1, m],
            device_id=(where, mate), device_id_type=MESH,
        )

    def b_copy(k):
        return pltpu.make_async_remote_copy(
            src_ref=b_ref, dst_ref=b_all.at[f], send_sem=b_send.at[k], recv_sem=b_recv.at[k],
            device_id=(where, (f + k) % shares), device_id_type=MESH,
        )

    chips = shares // 2
    x_copies = [x_copy(k) for k in range(1, parts)]
    first1 = [w_first(0, k1_ref, k1_all, m) for m in range(chips)]
    first2 = [w_first(1, k2_ref, k2_all, m) for m in range(chips)]
    second1 = [w_second(0, k1_all, m) for m in range(1, chips)]
    second2 = [w_second(1, k2_all, m) for m in range(1, chips)]
    b_copies = [b_copy(k) for k in range(1, shares)]
    own = [
        pltpu.make_async_copy(
            x_ref.at[:, :, pl.ds(pl.multiple_of(part * rows * SIDE, 128), span)],
            held.at[1 + side, f], own_sem.at[0],
        ),
        pltpu.make_async_copy(k1_ref, k1_all.at[f], own_sem.at[1]),
        pltpu.make_async_copy(k2_ref, k2_all.at[f], own_sem.at[2]),
        pltpu.make_async_copy(b_ref, b_all.at[f], own_sem.at[3]),
    ]
    for copy in x_copies + own + first1 + b_copies:
        copy.start()
    own[0].wait()
    for copy in x_copies:
        copy.wait_recv()

    def z_copy(up):
        return pltpu.make_async_remote_copy(
            src_ref=held.at[2 if up else 1], dst_ref=held.at[0 if up else 3],
            send_sem=z_send.at[int(up)], recv_sem=z_recv.at[int(up)],
            device_id=(where + PAIR if up else where - PAIR, f), device_id_type=MESH,
        )

    up_copy, down_copy = z_copy(True), z_copy(False)

    @pl.when(above)
    def _():
        up_copy.start()

    @pl.when(below)
    def _():
        down_copy.start()

    for copy in first2:
        copy.start()

    @pl.when(jnp.logical_not(below))
    def _():
        held[0] = jnp.zeros(held.shape[1:], held.dtype)

    @pl.when(jnp.logical_not(above))
    def _():
        held[3] = jnp.zeros(held.shape[1:], held.dtype)

    def turn(plane):
        block = jnp.concatenate(
            [held[plane // depth_planes, i, plane % depth_planes] for i in range(shares)], axis=0
        )
        spread(jnp.transpose(block.astype(jnp.float32)), taps1, plane)

    @pl.loop(depth_planes, 3 * depth_planes)
    def _(plane):
        turn(plane)

    for copy in first1:
        copy.wait_recv()
    for copy in second1:
        copy.start()

    @pl.when(below)
    def _():
        up_copy.wait_recv()

    @pl.when(above)
    def _():
        down_copy.wait_recv()

    @pl.loop(0, depth_planes)
    def _(plane):
        turn(plane)
        turn(plane + 3 * depth_planes)

    own[1].wait()
    own[3].wait()
    for copy in second1 + b_copies:
        copy.wait_recv()
    bias = jnp.sum(b_all[...], axis=0)
    wide = (rows + 2) * SIDE
    low_row = part * rows - 1
    low_plane = base * depth_planes - 1

    @pl.loop(0, planes + 2)
    def _(plane):
        hidden = activate(tap_sum(taps1, k1_all, shares, plane, wide), bias[0:1])
        row = low_row + lax.broadcasted_iota(jnp.int32, (wide, 1), 0) // SIDE
        deep = low_plane + plane
        usable = (row >= 0) & (row < SIDE) & (deep >= 0) & (deep < count * depth_planes)
        spread(jnp.where(usable, hidden, 0.0), taps2, plane)

    own[2].wait()
    for copy in first2:
        copy.wait_recv()
    for copy in second2:
        copy.start()
    for copy in second2:
        copy.wait_recv()
    cells = rows * SIDE
    share = results.shape[1] // shares

    def o_copy(plane, k):
        to = (f + k) % shares
        goal = (plane // depth_planes) * shares + to
        gap = (goal - part + parts) % parts
        level = plane % depth_planes
        lanes = pl.ds(pl.multiple_of(part * cells, 128), cells)
        source = results.at[plane, pl.ds(pl.multiple_of(to * share, share), share), :]
        remote = pltpu.make_async_remote_copy(
            src_ref=source, dst_ref=out_ref.at[level, :, lanes],
            send_sem=o_send.at[plane, k], recv_sem=o_recv.at[level, gap],
            device_id=home(goal), device_id_type=MESH,
        )
        local = pltpu.make_async_copy(source, out_ref.at[level, :, lanes], o_send.at[plane, k])
        return gap, remote, local

    @pl.loop(0, planes)
    def _(plane):
        done = activate(tap_sum(taps2, k2_all, shares, plane, cells), bias[1:2])
        results[plane] = jnp.transpose(done).astype(jnp.bfloat16)
        for k in range(shares):
            gap, remote, local = o_copy(plane, k)
            if k == 0:

                @pl.when(gap == 0)
                def _():
                    local.start()

                @pl.when(gap != 0)
                def _():
                    remote.start()

            else:
                remote.start()

    for level in range(depth_planes):
        for gap in range(1, parts):
            lanes = pl.ds(pl.multiple_of(((part - gap + parts) % parts) * cells, 128), cells)
            pltpu.make_async_remote_copy(
                src_ref=results.at[0, 0:share, :], dst_ref=out_ref.at[level, :, lanes],
                send_sem=o_send.at[0, 0], recv_sem=o_recv.at[level, gap],
                device_id=home((part + gap) % parts), device_id_type=MESH,
            ).wait_recv()
    for plane in range(planes):
        for k in range(shares):
            gap, remote, local = o_copy(plane, k)
            if k == 0:

                @pl.when(gap == 0)
                def _():
                    local.wait()

                @pl.when(gap != 0)
                def _():
                    remote.wait_send()

            else:
                remote.wait_send()
    for copy in x_copies + first1 + first2 + second1 + second2 + b_copies:
        copy.wait_send()

    @pl.when(above)
    def _():
        up_copy.wait_send()

    @pl.when(below)
    def _():
        down_copy.wait_send()


def joined(kernel_part):
    taps = kernel_part.reshape((9, 3) + kernel_part.shape[3:])
    return jnp.transpose(taps, (0, 2, 1, 3)).reshape(9, taps.shape[2], -1)


def local(features, first_kernel, first_bias, second_kernel, second_bias):
    shares = lax.axis_size("filt")
    count = lax.axis_size("depth")
    depth_planes, share, _ = features.shape
    parts = PAIR * shares
    rows = SIDE // parts
    planes = PAIR * depth_planes
    middle = first_kernel.shape[3] * shares
    channels = share * shares
    own_mid = first_kernel.shape[3]
    own_out = second_kernel.shape[3]
    framed = jnp.pad(features, ((0, 0), (0, 0), (REACH * SIDE, REACH * SIDE)))
    biases = jnp.zeros((8, middle), jnp.float32)
    both = jnp.stack([first_bias, second_bias])
    biases = lax.dynamic_update_slice(biases, both, (0, lax.axis_index("filt") * own_mid))
    span = (rows + 2 * REACH) * SIDE
    dma = pltpu.SemaphoreType.DMA
    return pl.pallas_call(
        functools.partial(kernel, shares, count, depth_planes),
        out_shape=jax.ShapeDtypeStruct((depth_planes, own_out, SIDE * SIDE), jnp.bfloat16),
        in_specs=[pl.BlockSpec(memory_space=pl.ANY)] * 4,
        out_specs=pl.BlockSpec(memory_space=pl.ANY),
        scratch_shapes=[
            pltpu.VMEM((4, shares, depth_planes, share, span), jnp.bfloat16),
            pltpu.VMEM((4 * depth_planes, span, 3 * channels), jnp.bfloat16),
            pltpu.VMEM((planes + 2, (rows + 2) * SIDE, 3 * middle), jnp.bfloat16),
            pltpu.VMEM((shares, 9, own_mid, 3 * channels), jnp.bfloat16),
            pltpu.VMEM((shares, 9, own_out, 3 * middle), jnp.bfloat16),
            pltpu.VMEM((shares, 8, middle), jnp.float32),
            pltpu.VMEM((planes, own_out * shares, rows * SIDE), jnp.bfloat16),
            dma((parts,)), dma((parts,)), dma((2,)), dma((2,)),
            dma((2, 2, shares // 2)), dma((2, 2, shares // 2)),
            dma((shares,)), dma((shares,)),
            dma((planes, shares)), dma((depth_planes, parts)), dma((4,)),
        ],
        compiler_params=pltpu.CompilerParams(
            collective_id=0, has_side_effects=True, vmem_limit_bytes=52 * 1024 * 1024
        ),
        cost_estimate=pl.CostEstimate(
            flops=20_000_000_000, bytes_accessed=10_000_000, transcendentals=0
        ),
    )(framed, joined(first_kernel), joined(second_kernel), biases)


def solution(mesh):
    in_specs = (
        P("depth", "filt", None),
        P(None, None, None, "filt", None),
        P("filt"),
        P(None, None, None, "filt", None),
        P("filt"),
    )
    out_specs = P("depth", "filt", None)
    return jax.shard_map(local, mesh=mesh, in_specs=in_specs, out_specs=out_specs, check_vma=False)
```

```python
import functools

import jax
import jax.numpy as jnp
from jax import lax
from jax.experimental import pallas as pl
from jax.experimental.pallas import tpu as pltpu
from jax.sharding import PartitionSpec as P

SIDE = 64
REACH = 2
PAIR = 2
MESH = pl.DeviceIdType.MESH


leak_slope = 0.3


def activate(summed, bias):
    shifted = summed + bias
    return jnp.where(shifted > 0, shifted, leak_slope * shifted)


def spread(values, buffer, plane):
    cells, channels = values.shape
    column = lax.broadcasted_iota(jnp.int32, (cells, 1), 0) % SIDE
    before = jnp.where(column > 0, pltpu.roll(values, 1, 0), 0.0)
    after = jnp.where(column < SIDE - 1, pltpu.roll(values, cells - 1, 0), 0.0)
    buffer[plane, :, 0:channels] = before.astype(jnp.bfloat16)
    buffer[plane, :, channels : 2 * channels] = values.astype(jnp.bfloat16)
    buffer[plane, :, 2 * channels : 3 * channels] = after.astype(jnp.bfloat16)


def tap_sum(buffer, kernels, shares, plane, cells):
    window = jnp.concatenate(
        [
            buffer[plane + tap_d, tap_h * SIDE : tap_h * SIDE + cells, :]
            for tap_d in range(3)
            for tap_h in range(3)
        ],
        axis=1,
    )
    weights = jnp.concatenate(
        [
            jnp.concatenate([kernels[i, tap, half] for tap in range(27)], axis=1)
            for i in range(shares)
            for half in range(2)
        ],
        axis=0,
    )
    return lax.dot_general(
        window, weights, (((1,), (1,)), ((), ())), preferred_element_type=jnp.float32
    )


def kernel(
    shares, count, depth_planes,
    x_ref, k1_ref, k2_ref, b_ref, out_ref,
    held, taps1, taps2, k1_all, k2_all, b_all, results,
    x_send, x_recv, z_send, z_recv, w_send, w_recv, b_send, b_recv, o_send, o_recv, own_sem,
):
    parts = PAIR * shares
    rows = SIDE // parts
    span = (rows + 2 * REACH) * SIDE
    planes = PAIR * depth_planes
    where = lax.axis_index("depth")
    f = lax.axis_index("filt")
    base = (where // PAIR) * PAIR
    side = where % PAIR
    part = side * shares + f
    mate = f + 1 - 2 * (f % 2)
    below = where >= PAIR
    above = where < count - PAIR

    def home(other):
        return (base + other // shares, other % shares)

    barrier = pltpu.get_barrier_semaphore()
    for k in range(1, parts):
        pl.semaphore_signal(barrier, inc=1, device_id=home((part + k) % parts), device_id_type=MESH)

    @pl.when(below)
    def _():
        pl.semaphore_signal(barrier, inc=1, device_id=(where - PAIR, f), device_id_type=MESH)

    @pl.when(above)
    def _():
        pl.semaphore_signal(barrier, inc=1, device_id=(where + PAIR, f), device_id_type=MESH)

    pl.semaphore_wait(barrier, parts - 1 + below.astype(jnp.int32) + above.astype(jnp.int32))

    def x_copy(k):
        to = (part + k) % parts
        return pltpu.make_async_remote_copy(
            src_ref=x_ref.at[:, :, pl.ds(pl.multiple_of(to * rows * SIDE, 128), span)],
            dst_ref=held.at[1 + side, f],
            send_sem=x_send.at[k], recv_sem=x_recv.at[k],
            device_id=home(to), device_id_type=MESH,
        )

    def w_copy(layer, stage, m, source_ref, dest_ref, to):
        return pltpu.make_async_remote_copy(
            src_ref=source_ref, dst_ref=dest_ref,
            send_sem=w_send.at[layer, stage, m], recv_sem=w_recv.at[layer, stage, m],
            device_id=to, device_id_type=MESH,
        )

    twin = base + 1 - side

    def w_whole(layer, ref, dest):
        return w_copy(layer, 0, 0, ref, dest.at[f], (where, mate))

    def w_half(layer, ref, dest, m):
        return w_copy(
            layer, 0, m, ref.at[:, side], dest.at[f, :, side], (where, (f + 2 * m) % shares)
        )

    def w_pass(layer, stage, dest, m):
        source = (f - 2 * m + shares) % shares
        piece = dest.at[source, :, (1 - side) if stage == 3 else side]
        return w_copy(layer, stage, m, piece, piece, (twin, f) if stage == 1 else (where, mate))

    def b_copy(k):
        return pltpu.make_async_remote_copy(
            src_ref=b_ref, dst_ref=b_all.at[f], send_sem=b_send.at[k], recv_sem=b_recv.at[k],
            device_id=(where, (f + k) % shares), device_id_type=MESH,
        )

    chips = shares // 2
    x_copies = [x_copy(k) for k in range(1, parts)]
    far = range(1, chips)
    mates = [w_whole(0, k1_ref, k1_all), w_whole(1, k2_ref, k2_all)]
    halves1 = [w_half(0, k1_ref, k1_all, m) for m in far]
    halves2 = [w_half(1, k2_ref, k2_all, m) for m in far]
    passes1 = [[w_pass(0, stage, k1_all, m) for m in far] for stage in (1, 2, 3)]
    passes2 = [[w_pass(1, stage, k2_all, m) for m in far] for stage in (1, 2, 3)]
    b_copies = [b_copy(k) for k in range(1, shares)]
    own = [
        pltpu.make_async_copy(
            x_ref.at[:, :, pl.ds(pl.multiple_of(part * rows * SIDE, 128), span)],
            held.at[1 + side, f], own_sem.at[0],
        ),
        pltpu.make_async_copy(k1_ref, k1_all.at[f], own_sem.at[1]),
        pltpu.make_async_copy(k2_ref, k2_all.at[f], own_sem.at[2]),
        pltpu.make_async_copy(b_ref, b_all.at[f], own_sem.at[3]),
    ]
    for copy in x_copies + own + halves1 + mates[:1] + b_copies:
        copy.start()
    own[0].wait()
    for copy in x_copies:
        copy.wait_recv()

    def z_copy(up):
        return pltpu.make_async_remote_copy(
            src_ref=held.at[2 if up else 1], dst_ref=held.at[0 if up else 3],
            send_sem=z_send.at[int(up)], recv_sem=z_recv.at[int(up)],
            device_id=(where + PAIR if up else where - PAIR, f), device_id_type=MESH,
        )

    up_copy, down_copy = z_copy(True), z_copy(False)

    @pl.when(above)
    def _():
        up_copy.start()

    @pl.when(below)
    def _():
        down_copy.start()

    for copy in halves2 + mates[1:]:
        copy.start()

    @pl.when(jnp.logical_not(below))
    def _():
        held[0] = jnp.zeros(held.shape[1:], held.dtype)

    @pl.when(jnp.logical_not(above))
    def _():
        held[3] = jnp.zeros(held.shape[1:], held.dtype)

    def turn(plane):
        block = jnp.concatenate(
            [held[plane // depth_planes, i, plane % depth_planes] for i in range(shares)], axis=0
        )
        spread(jnp.transpose(block.astype(jnp.float32)), taps1, plane)

    @pl.loop(depth_planes, 3 * depth_planes)
    def _(plane):
        turn(plane)

    def relay(halves, passes):
        for copy in halves:
            copy.wait_recv()
        for copy in passes[0] + passes[1]:
            copy.start()

    def finish(passes):
        for copy in passes[0]:
            copy.wait_recv()
        for copy in passes[2]:
            copy.start()
        for copy in passes[1] + passes[2]:
            copy.wait_recv()

    relay(halves1, passes1)
    own[1].wait()
    own[3].wait()
    for copy in b_copies + mates[:1]:
        copy.wait_recv()
    finish(passes1)
    bias = jnp.sum(b_all[...], axis=0)
    wide = (rows + 2) * SIDE
    low_row = part * rows - 1
    low_plane = base * depth_planes - 1

    @pl.loop(0, planes + 2)
    def _(step):
        @pl.when(step == 2)
        def _():
            @pl.when(below)
            def _():
                up_copy.wait_recv()

            @pl.when(above)
            def _():
                down_copy.wait_recv()

            @pl.loop(0, 2 * depth_planes)
            def _(i):
                turn((i // depth_planes) * (2 * depth_planes) + i)

        @pl.when(step == 4)
        def _():
            relay(halves2, passes2)

        plane = (step + 2) % 4 + 2 * (step // 4)
        hidden = activate(tap_sum(taps1, k1_all, shares, plane, wide), bias[0:1])
        row = low_row + lax.broadcasted_iota(jnp.int32, (wide, 1), 0) // SIDE
        deep = low_plane + plane
        usable = (row >= 0) & (row < SIDE) & (deep >= 0) & (deep < count * depth_planes)
        spread(jnp.where(usable, hidden, 0.0), taps2, plane)

    own[2].wait()
    for copy in mates[1:]:
        copy.wait_recv()
    finish(passes2)
    cells = rows * SIDE
    share = results.shape[1] // shares

    def o_copy(plane, k):
        to = (f + k) % shares
        goal = (plane // depth_planes) * shares + to
        gap = (goal - part + parts) % parts
        level = plane % depth_planes
        lanes = pl.ds(pl.multiple_of(part * cells, 128), cells)
        source = results.at[plane, pl.ds(pl.multiple_of(to * share, share), share), :]

        def remote():
            return pltpu.make_async_remote_copy(
                src_ref=source, dst_ref=out_ref.at[level, :, lanes],
                send_sem=o_send.at[plane, k], recv_sem=o_recv.at[level, gap],
                device_id=home(goal), device_id_type=MESH,
            )

        def local():
            return pltpu.make_async_copy(source, out_ref.at[level, :, lanes], o_send.at[plane, k])

        return gap, remote, local

    @pl.loop(0, planes)
    def _(plane):
        done = activate(tap_sum(taps2, k2_all, shares, plane, cells), bias[1:2])
        results[plane] = jnp.transpose(done).astype(jnp.bfloat16)
        for k in range(shares):
            gap, remote, local = o_copy(plane, k)
            if k == 0:

                @pl.when(gap == 0)
                def _():
                    local().start()

                @pl.when(gap != 0)
                def _():
                    remote().start()

            else:
                remote().start()

    for level in range(depth_planes):
        for gap in range(1, parts):
            lanes = pl.ds(pl.multiple_of(((part - gap + parts) % parts) * cells, 128), cells)
            pltpu.make_async_remote_copy(
                src_ref=results.at[0, 0:share, :], dst_ref=out_ref.at[level, :, lanes],
                send_sem=o_send.at[0, 0], recv_sem=o_recv.at[level, gap],
                device_id=home((part + gap) % parts), device_id_type=MESH,
            ).wait_recv()
    for plane in range(planes):
        for k in range(shares):
            gap, remote, local = o_copy(plane, k)
            if k == 0:

                @pl.when(gap == 0)
                def _():
                    local().wait()

                @pl.when(gap != 0)
                def _():
                    remote().wait_send()

            else:
                remote().wait_send()
    for copy in x_copies + mates + halves1 + halves2 + sum(passes1 + passes2, []) + b_copies:
        copy.wait_send()

    @pl.when(above)
    def _():
        up_copy.wait_send()

    @pl.when(below)
    def _():
        down_copy.wait_send()


def halved(kernel_part):
    return kernel_part.reshape(27, 2, kernel_part.shape[3] // 2, kernel_part.shape[4])


def local(features, first_kernel, first_bias, second_kernel, second_bias):
    shares = lax.axis_size("filt")
    count = lax.axis_size("depth")
    depth_planes, share, _ = features.shape
    parts = PAIR * shares
    rows = SIDE // parts
    planes = PAIR * depth_planes
    middle = first_kernel.shape[3] * shares
    channels = share * shares
    own_mid = first_kernel.shape[3]
    own_out = second_kernel.shape[3]
    framed = jnp.pad(features, ((0, 0), (0, 0), (REACH * SIDE, REACH * SIDE)))
    biases = jnp.zeros((8, middle), jnp.float32)
    both = jnp.stack([first_bias, second_bias])
    biases = lax.dynamic_update_slice(biases, both, (0, lax.axis_index("filt") * own_mid))
    span = (rows + 2 * REACH) * SIDE
    dma = pltpu.SemaphoreType.DMA
    return pl.pallas_call(
        functools.partial(kernel, shares, count, depth_planes),
        out_shape=jax.ShapeDtypeStruct((depth_planes, own_out, SIDE * SIDE), jnp.bfloat16),
        in_specs=[pl.BlockSpec(memory_space=pl.ANY)] * 4,
        out_specs=pl.BlockSpec(memory_space=pl.ANY),
        scratch_shapes=[
            pltpu.VMEM((4, shares, depth_planes, share, span), jnp.bfloat16),
            pltpu.VMEM((4 * depth_planes, span, 3 * channels), jnp.bfloat16),
            pltpu.VMEM((planes + 2, (rows + 2) * SIDE, 3 * middle), jnp.bfloat16),
            pltpu.VMEM((shares, 27, 2, own_mid // 2, channels), jnp.bfloat16),
            pltpu.VMEM((shares, 27, 2, own_out // 2, middle), jnp.bfloat16),
            pltpu.VMEM((shares, 8, middle), jnp.float32),
            pltpu.VMEM((planes, own_out * shares, rows * SIDE), jnp.bfloat16),
            dma((parts,)), dma((parts,)), dma((2,)), dma((2,)),
            dma((2, 4, shares // 2)), dma((2, 4, shares // 2)),
            dma((shares,)), dma((shares,)),
            dma((planes, shares)), dma((depth_planes, parts)), dma((4,)),
        ],
        compiler_params=pltpu.CompilerParams(
            collective_id=0, has_side_effects=True, vmem_limit_bytes=52 * 1024 * 1024
        ),
        cost_estimate=pl.CostEstimate(
            flops=20_000_000_000, bytes_accessed=10_000_000, transcendentals=0
        ),
    )(framed, halved(first_kernel), halved(second_kernel), biases)


def solution(mesh):
    in_specs = (
        P("depth", "filt", None),
        P(None, None, None, "filt", None),
        P("filt"),
        P(None, None, None, "filt", None),
        P("filt"),
    )
    out_specs = P("depth", "filt", None)
    return jax.shard_map(local, mesh=mesh, in_specs=in_specs, out_specs=out_specs, check_vma=False)
```

```python
import functools

import jax
import jax.numpy as jnp
from jax import lax
from jax.experimental import pallas as pl
from jax.experimental.pallas import tpu as pltpu
from jax.sharding import PartitionSpec as P

SIDE = 64
REACH = 2
PAIR = 2
MESH = pl.DeviceIdType.MESH


leak_slope = 0.3


def activate(summed, bias):
    shifted = summed + bias
    return jnp.where(shifted > 0, shifted, leak_slope * shifted)


def spread(values, buffer, plane):
    cells, channels = values.shape
    column = lax.broadcasted_iota(jnp.int32, (cells, 1), 0) % SIDE
    before = jnp.where(column > 0, pltpu.roll(values, 1, 0), 0.0)
    after = jnp.where(column < SIDE - 1, pltpu.roll(values, cells - 1, 0), 0.0)
    buffer[plane, :, 0:channels] = before.astype(jnp.bfloat16)
    buffer[plane, :, channels : 2 * channels] = values.astype(jnp.bfloat16)
    buffer[plane, :, 2 * channels : 3 * channels] = after.astype(jnp.bfloat16)


def tap_sum(buffer, kernels, shares, plane, cells):
    window = jnp.concatenate(
        [
            buffer[plane + tap_d, tap_h * SIDE : tap_h * SIDE + cells, :]
            for tap_d in range(3)
            for tap_h in range(3)
        ],
        axis=1,
    )
    weights = jnp.concatenate(
        [
            jnp.concatenate([kernels[i, tap, half] for tap in range(27)], axis=1)
            for i in range(shares)
            for half in range(2)
        ],
        axis=0,
    )
    return lax.dot_general(
        window, weights, (((1,), (1,)), ((), ())), preferred_element_type=jnp.float32
    )


def kernel(
    shares, count, depth_planes,
    x_ref, k1_ref, k2_ref, b_ref, out_ref,
    held, taps1, taps2, k1_all, k2_all, b_all, results,
    x_send, x_recv, z_send, z_recv, w_send, w_recv, b_send, b_recv, o_send, o_recv, own_sem,
):
    parts = PAIR * shares
    rows = SIDE // parts
    span = (rows + 2 * REACH) * SIDE
    planes = PAIR * depth_planes
    where = lax.axis_index("depth")
    f = lax.axis_index("filt")
    base = (where // PAIR) * PAIR
    side = where % PAIR
    part = side * shares + f
    mate = f + 1 - 2 * (f % 2)
    below = where >= PAIR
    above = where < count - PAIR

    def home(other):
        return (base + other // shares, other % shares)

    barrier = pltpu.get_barrier_semaphore()
    for k in range(1, parts):
        pl.semaphore_signal(barrier, inc=1, device_id=home((part + k) % parts), device_id_type=MESH)

    @pl.when(below)
    def _():
        pl.semaphore_signal(barrier, inc=1, device_id=(where - PAIR, f), device_id_type=MESH)

    @pl.when(above)
    def _():
        pl.semaphore_signal(barrier, inc=1, device_id=(where + PAIR, f), device_id_type=MESH)

    pl.semaphore_wait(barrier, parts - 1 + below.astype(jnp.int32) + above.astype(jnp.int32))

    def x_copy(k):
        to = (part + k) % parts
        return pltpu.make_async_remote_copy(
            src_ref=x_ref.at[:, :, pl.ds(pl.multiple_of(to * rows * SIDE, 128), span)],
            dst_ref=held.at[1 + side, f],
            send_sem=x_send.at[k], recv_sem=x_recv.at[k],
            device_id=home(to), device_id_type=MESH,
        )

    def w_copy(layer, stage, m, source_ref, dest_ref, to):
        return pltpu.make_async_remote_copy(
            src_ref=source_ref, dst_ref=dest_ref,
            send_sem=w_send.at[layer, stage, m], recv_sem=w_recv.at[layer, stage, m],
            device_id=to, device_id_type=MESH,
        )

    twin = base + 1 - side

    def w_whole(layer, ref, dest):
        return w_copy(layer, 0, 0, ref, dest.at[f], (where, mate))

    def w_half(layer, ref, dest, m):
        return w_copy(
            layer, 0, m, ref.at[:, side], dest.at[f, :, side], (where, (f + 2 * m) % shares)
        )

    def w_pass(layer, stage, dest, m):
        source = (f - 2 * m + shares) % shares
        piece = dest.at[source, :, (1 - side) if stage == 3 else side]
        return w_copy(layer, stage, m, piece, piece, (twin, f) if stage == 1 else (where, mate))

    def b_copy(k):
        return pltpu.make_async_remote_copy(
            src_ref=b_ref, dst_ref=b_all.at[f], send_sem=b_send.at[k], recv_sem=b_recv.at[k],
            device_id=(where, (f + k) % shares), device_id_type=MESH,
        )

    chips = shares // 2
    x_copies = [x_copy(k) for k in range(1, parts)]
    far = range(1, chips)
    mates = [w_whole(0, k1_ref, k1_all), w_whole(1, k2_ref, k2_all)]
    halves1 = [w_half(0, k1_ref, k1_all, m) for m in far]
    halves2 = [w_half(1, k2_ref, k2_all, m) for m in far]
    passes1 = [[w_pass(0, stage, k1_all, m) for m in far] for stage in (1, 2, 3)]
    passes2 = [[w_pass(1, stage, k2_all, m) for m in far] for stage in (1, 2, 3)]
    b_copies = [b_copy(k) for k in range(1, shares)]
    own = [
        pltpu.make_async_copy(
            x_ref.at[:, :, pl.ds(pl.multiple_of(part * rows * SIDE, 128), span)],
            held.at[1 + side, f], own_sem.at[0],
        ),
        pltpu.make_async_copy(k1_ref, k1_all.at[f], own_sem.at[1]),
        pltpu.make_async_copy(k2_ref, k2_all.at[f], own_sem.at[2]),
        pltpu.make_async_copy(b_ref, b_all.at[f], own_sem.at[3]),
    ]
    for copy in x_copies + own + halves1 + halves2 + mates + b_copies:
        copy.start()
    own[0].wait()
    for copy in x_copies:
        copy.wait_recv()

    def z_copy(up):
        return pltpu.make_async_remote_copy(
            src_ref=held.at[2 if up else 1], dst_ref=held.at[0 if up else 3],
            send_sem=z_send.at[int(up)], recv_sem=z_recv.at[int(up)],
            device_id=(where + PAIR if up else where - PAIR, f), device_id_type=MESH,
        )

    up_copy, down_copy = z_copy(True), z_copy(False)

    @pl.when(above)
    def _():
        up_copy.start()

    @pl.when(below)
    def _():
        down_copy.start()

    @pl.when(jnp.logical_not(below))
    def _():
        held[0] = jnp.zeros(held.shape[1:], held.dtype)

    @pl.when(jnp.logical_not(above))
    def _():
        held[3] = jnp.zeros(held.shape[1:], held.dtype)

    def turn(plane):
        block = jnp.concatenate(
            [held[plane // depth_planes, i, plane % depth_planes] for i in range(shares)], axis=0
        )
        spread(jnp.transpose(block.astype(jnp.float32)), taps1, plane)

    @pl.loop(depth_planes, 3 * depth_planes)
    def _(plane):
        turn(plane)

    def relay(halves, passes):
        for copy in halves:
            copy.wait_recv()
        for copy in passes[0] + passes[1]:
            copy.start()

    def finish(passes):
        for copy in passes[0]:
            copy.wait_recv()
        for copy in passes[2]:
            copy.start()
        for copy in passes[1] + passes[2]:
            copy.wait_recv()

    relay(halves1, passes1)
    own[1].wait()
    own[3].wait()
    for copy in b_copies + mates[:1]:
        copy.wait_recv()
    finish(passes1)
    bias = jnp.sum(b_all[...], axis=0)
    wide = (rows + 2) * SIDE
    low_row = part * rows - 1
    low_plane = base * depth_planes - 1

    @pl.loop(0, planes + 2)
    def _(step):
        @pl.when(step == 2)
        def _():
            @pl.when(below)
            def _():
                up_copy.wait_recv()

            @pl.when(above)
            def _():
                down_copy.wait_recv()

            @pl.loop(0, 2 * depth_planes)
            def _(i):
                turn((i // depth_planes) * (2 * depth_planes) + i)

        @pl.when(step == 4)
        def _():
            relay(halves2, passes2)

        plane = (step + 2) % 4 + 2 * (step // 4)
        hidden = activate(tap_sum(taps1, k1_all, shares, plane, wide), bias[0:1])
        row = low_row + lax.broadcasted_iota(jnp.int32, (wide, 1), 0) // SIDE
        deep = low_plane + plane
        usable = (row >= 0) & (row < SIDE) & (deep >= 0) & (deep < count * depth_planes)
        spread(jnp.where(usable, hidden, 0.0), taps2, plane)

    own[2].wait()
    for copy in mates[1:]:
        copy.wait_recv()
    finish(passes2)
    cells = rows * SIDE
    share = results.shape[1] // shares

    def o_copy(plane, k):
        to = (f + k) % shares
        goal = (plane // depth_planes) * shares + to
        gap = (goal - part + parts) % parts
        level = plane % depth_planes
        lanes = pl.ds(pl.multiple_of(part * cells, 128), cells)
        source = results.at[plane, pl.ds(pl.multiple_of(to * share, share), share), :]

        def remote():
            return pltpu.make_async_remote_copy(
                src_ref=source, dst_ref=out_ref.at[level, :, lanes],
                send_sem=o_send.at[plane, k], recv_sem=o_recv.at[level, gap],
                device_id=home(goal), device_id_type=MESH,
            )

        def local():
            return pltpu.make_async_copy(source, out_ref.at[level, :, lanes], o_send.at[plane, k])

        return gap, remote, local

    @pl.loop(0, planes)
    def _(plane):
        done = activate(tap_sum(taps2, k2_all, shares, plane, cells), bias[1:2])
        results[plane] = jnp.transpose(done).astype(jnp.bfloat16)
        for k in range(shares):
            gap, remote, local = o_copy(plane, k)
            if k == 0:

                @pl.when(gap == 0)
                def _():
                    local().start()

                @pl.when(gap != 0)
                def _():
                    remote().start()

            else:
                remote().start()

    for level in range(depth_planes):
        for gap in range(1, parts):
            lanes = pl.ds(pl.multiple_of(((part - gap + parts) % parts) * cells, 128), cells)
            pltpu.make_async_remote_copy(
                src_ref=results.at[0, 0:share, :], dst_ref=out_ref.at[level, :, lanes],
                send_sem=o_send.at[0, 0], recv_sem=o_recv.at[level, gap],
                device_id=home((part + gap) % parts), device_id_type=MESH,
            ).wait_recv()
    for plane in range(planes):
        for k in range(shares):
            gap, remote, local = o_copy(plane, k)
            if k == 0:

                @pl.when(gap == 0)
                def _():
                    local().wait()

                @pl.when(gap != 0)
                def _():
                    remote().wait_send()

            else:
                remote().wait_send()
    for copy in x_copies + mates + halves1 + halves2 + sum(passes1 + passes2, []) + b_copies:
        copy.wait_send()

    @pl.when(above)
    def _():
        up_copy.wait_send()

    @pl.when(below)
    def _():
        down_copy.wait_send()


def halved(kernel_part):
    return kernel_part.reshape(27, 2, kernel_part.shape[3] // 2, kernel_part.shape[4])


def local(features, first_kernel, first_bias, second_kernel, second_bias):
    shares = lax.axis_size("filt")
    count = lax.axis_size("depth")
    depth_planes, share, _ = features.shape
    parts = PAIR * shares
    rows = SIDE // parts
    planes = PAIR * depth_planes
    middle = first_kernel.shape[3] * shares
    channels = share * shares
    own_mid = first_kernel.shape[3]
    own_out = second_kernel.shape[3]
    framed = jnp.pad(features, ((0, 0), (0, 0), (REACH * SIDE, REACH * SIDE)))
    biases = jnp.zeros((8, middle), jnp.float32)
    both = jnp.stack([first_bias, second_bias])
    biases = lax.dynamic_update_slice(biases, both, (0, lax.axis_index("filt") * own_mid))
    span = (rows + 2 * REACH) * SIDE
    dma = pltpu.SemaphoreType.DMA
    return pl.pallas_call(
        functools.partial(kernel, shares, count, depth_planes),
        out_shape=jax.ShapeDtypeStruct((depth_planes, own_out, SIDE * SIDE), jnp.bfloat16),
        in_specs=[pl.BlockSpec(memory_space=pl.ANY)] * 4,
        out_specs=pl.BlockSpec(memory_space=pl.ANY),
        scratch_shapes=[
            pltpu.VMEM((4, shares, depth_planes, share, span), jnp.bfloat16),
            pltpu.VMEM((4 * depth_planes, span, 3 * channels), jnp.bfloat16),
            pltpu.VMEM((planes + 2, (rows + 2) * SIDE, 3 * middle), jnp.bfloat16),
            pltpu.VMEM((shares, 27, 2, own_mid // 2, channels), jnp.bfloat16),
            pltpu.VMEM((shares, 27, 2, own_out // 2, middle), jnp.bfloat16),
            pltpu.VMEM((shares, 8, middle), jnp.float32),
            pltpu.VMEM((planes, own_out * shares, rows * SIDE), jnp.bfloat16),
            dma((parts,)), dma((parts,)), dma((2,)), dma((2,)),
            dma((2, 4, shares // 2)), dma((2, 4, shares // 2)),
            dma((shares,)), dma((shares,)),
            dma((planes, shares)), dma((depth_planes, parts)), dma((4,)),
        ],
        compiler_params=pltpu.CompilerParams(
            collective_id=0, has_side_effects=True, vmem_limit_bytes=52 * 1024 * 1024
        ),
        cost_estimate=pl.CostEstimate(
            flops=20_000_000_000, bytes_accessed=10_000_000, transcendentals=0
        ),
    )(framed, halved(first_kernel), halved(second_kernel), biases)


def solution(mesh):
    in_specs = (
        P("depth", "filt", None),
        P(None, None, None, "filt", None),
        P("filt"),
        P(None, None, None, "filt", None),
        P("filt"),
    )
    out_specs = P("depth", "filt", None)
    return jax.shard_map(local, mesh=mesh, in_specs=in_specs, out_specs=out_specs, check_vma=False)
```
